512 devices in a mesh: seq: 32 (over x, z_hi, core), chan: 16 (over y, z_lo).
Axes of the slice: x: 4, y: 4, z: 16 (z_hi: 4, z_lo: 4; z = z_hi * 4 + z_lo), core: 2. Of those that a mesh axis runs over, the one named last changes fastest.
Arguments:
- values: bfloat16 [4096, 16384], P('chan', 'seq'), may hold values from -6 to 6
- gates: bfloat16 [4096, 16384], P('chan', 'seq'), may hold values from -6 to 6
- skip_gain: float32 [4096], P('chan'), may hold values from 0.3 to 3
- filters: bfloat16 [4096, 16384], P('chan', 'seq'), may hold values from -6 to 6
- out_weight: bfloat16 [4096, 4096], P('seq', 'chan'), may hold values from -0.09375 to 0.09375
Outputs:
- projected: bfloat16 [4096, 16384], P('chan', 'seq')
The draws below stay inside these ranges and needn't reach their ends.
All inputs are finite; a program needn't handle non-finite values.
Results may differ from the reference program's by a relative error of at most 0.0052.
Values may be sent and summed in bfloat16 or wider, within the bound.
A program may use at most 64 MiB of HBM per device.

```python
import math
import jax
import jax.numpy as jnp
from jax import lax

D = 4096
LEN = 16384


def draw_filters(key, part):
    key = jax.random.fold_in(key, 7)
    rate_key, noise_key, reach_key = jax.random.split(key, 3)
    low_rate = jnp.log(jnp.float32(0.3))
    high_rate = jnp.log(jnp.float32(LEN / 40.0))
    rate = jnp.exp(jax.random.uniform(rate_key, (D, 1), jnp.float32, low_rate, high_rate))
    steps_along = jnp.arange(LEN, dtype=jnp.float32)[None, :]
    envelope = jnp.exp(-rate * steps_along / LEN) * jnp.sqrt(2.0 * rate / (LEN * (1.0 - jnp.exp(-2.0 * rate))))
    reach = jnp.exp(jax.random.uniform(reach_key, (D, 1), jnp.float32, jnp.log(jnp.float32(0.2)), jnp.log(jnp.float32(0.3))))
    amplitude = envelope + reach / jnp.sqrt(jnp.float32(LEN))
    noise = jax.random.normal(noise_key, (D, LEN), jnp.float32)
    return jnp.clip(noise * amplitude, -6.0, 6.0).astype(jnp.bfloat16)


def steps_of(rng, dims, shards, low, high):
    def one(position, shards_of):
        heights = jax.random.uniform(jax.random.fold_in(jax.random.fold_in(rng, 6), position), (shards_of,), jnp.float32, low / len(shards), high / len(shards))
        return jnp.repeat(jnp.exp(heights), dims[position] // shards_of).reshape((-1,) + (1,) * (len(dims) - position - 1))

    level = one(*shards[0])
    for cut in shards[1:]:
        level = level * one(*cut)
    return level


def scatter_about(key, extent, width, most, pieces=(), kind=jnp.bfloat16):
    values = width * jax.random.normal(key, extent, jnp.float32)
    if pieces:
        values = values * steps_of(key, extent, pieces, -0.22, 0.18)
    return jnp.clip(values, -most, most).astype(kind)


def setup_inputs(seed: int = 0) -> dict:
    streams_of = jax.random.split(jax.random.key(seed), 6)
    values = scatter_about(streams_of[0], (D, LEN), 1.0, 6.0, ((0, 16), (1, 32)))
    gates = scatter_about(streams_of[1], (D, LEN), 1.0, 6.0, ((0, 16), (1, 32)))
    skip_gain = jnp.clip(jnp.exp(math.log(3.0) - 2.3025851 * jax.random.uniform(streams_of[2], (D,), jnp.float32) ** steps_of(streams_of[2], (D,), ((0, 16),), -0.2, 0.2)), 0.3, 3.0)
    filters = draw_filters(jax.random.fold_in(streams_of[5], 71), 0)
    out_weight = scatter_about(streams_of[4], (D, D), D ** -0.5, 0.09375, ((0, 32), (1, 16)))
    return {"values": values, "gates": gates, "skip_gain": skip_gain, "filters": filters, "out_weight": out_weight}


def filter_block(operands):
    signal, kernel = operands
    sample_count = signal.shape[1]
    period_length = 2 * sample_count
    transformed = jnp.fft.rfft(signal, n=period_length, axis=1)
    response = jnp.fft.rfft(kernel, n=period_length, axis=1)
    inverse = jnp.fft.irfft(response * transformed, n=period_length, axis=1)
    return inverse[:, :sample_count]


def reference(values, gates, skip_gain, filters, out_weight):
    block_count = D // 64
    signal = values.astype(jnp.float32).reshape(block_count, 64, LEN)
    kernel = filters.astype(jnp.float32).reshape(block_count, 64, LEN)
    filtered = lax.map(filter_block, (signal, kernel)).reshape(D, LEN)
    rounded = lax.optimization_barrier(filtered.astype(jnp.bfloat16)).astype(jnp.float32)
    mixed = (gates.astype(jnp.float32) * (rounded + skip_gain[:, None] * values.astype(jnp.float32))).astype(jnp.bfloat16)
    return jnp.dot(out_weight.T, mixed, preferred_element_type=jnp.float32).astype(jnp.bfloat16)
```

```python
import functools

import jax
import jax.numpy as jnp
from jax import lax
from jax.experimental import pallas as pl
from jax.experimental.pallas import tpu as pltpu
from jax.sharding import PartitionSpec as P

MESH = pl.DeviceIdType.MESH
VMEM = pltpu.VMEM
BF16 = jnp.bfloat16
F32 = jnp.float32

NX, NZ, NC = 4, 4, 2
SEQ = NX * NZ * NC
NY, NL = 4, 4
LANES = 128
ROWS = 4
CH = 8


def mod(a, n):
    return lax.rem(a, n)


def seq_coords():
    s = lax.axis_index("seq")
    return s, lax.div(s, NZ * NC), mod(lax.div(s, NC), NZ), mod(s, NC)


def seq_id(x, z, c):
    return x * (NZ * NC) + z * NC + c


def signal(sem, seq, chan):
    pl.semaphore_signal(sem, inc=1, device_id={"seq": seq, "chan": chan}, device_id_type=MESH)


def remote(src, dst, ssem, rsem, seq, chan):
    return pltpu.make_async_remote_copy(
        src_ref=src, dst_ref=dst, send_sem=ssem, recv_sem=rsem,
        device_id={"seq": seq, "chan": chan}, device_id_type=MESH)


def scatter_kernel(v_ref, f_ref, got, out, ssem, rsem):
    me, x, z, c = seq_coords()
    chan = lax.axis_index("chan")
    barrier = pltpu.get_barrier_semaphore()

    def hello(k, _):
        signal(barrier, mod(me + k, SEQ), chan)
        return 0

    lax.fori_loop(1, SEQ, hello, 0)

    def pack(g, _):
        for ref, base in ((v_ref, 0), (f_ref, ROWS * CH)):
            block = ref[pl.ds(pl.multiple_of(16 * g, 16), 16), :].astype(F32)
            for half in range(2):
                part = block[CH * half:CH * (half + 1)]
                rows = [part[:, LANES * p:LANES * (p + 1)] for p in range(ROWS)]
                out[2 * g + half, base:base + ROWS * CH, :] = jnp.concatenate(rows, 0).astype(BF16)
        return 0

    lax.fori_loop(0, SEQ // 2, pack, 0)
    pl.semaphore_wait(barrier, SEQ - 1)

    def partner(dz, j, sign):
        dx, dc = lax.div(j, NC), mod(j, NC)
        return seq_id(mod(x + sign * dx + NX, NX), mod(z + sign * dz + NZ, NZ), mod(c + dc, NC))

    for dz in (2, 1, 3, 0):
        def send(j, _, dz=dz):
            to = partner(dz, j, 1)
            remote(out.at[to], got.at[me], ssem.at[to], rsem.at[me], to, chan).start()
            return 0

        lax.fori_loop(0 if dz else 1, NX * NC, send, 0)
    got[me] = out[me]
    for dz in (0, 1, 3, 2):
        def finish(j, _, dz=dz):
            to = partner(dz, j, 1)
            remote(out.at[to], got.at[to], ssem.at[to], rsem.at[to], to, chan).wait()
            return 0

        lax.fori_loop(0 if dz else 1, NX * NC, finish, 0)


def scatter(values, filters):
    return pl.pallas_call(
        scatter_kernel,
        out_shape=jax.ShapeDtypeStruct((SEQ, 2 * ROWS * CH, LANES), BF16),
        in_specs=[pl.BlockSpec(memory_space=VMEM)] * 2,
        out_specs=pl.BlockSpec(memory_space=VMEM),
        scratch_shapes=[
            VMEM((SEQ, 2 * ROWS * CH, LANES), BF16),
            pltpu.SemaphoreType.DMA((SEQ,)),
            pltpu.SemaphoreType.DMA((SEQ,)),
        ],
        compiler_params=pltpu.CompilerParams(
            collective_id=1, has_side_effects=True, vmem_limit_bytes=16 * 2**20),
        name="scatter_tokens",
    )(values, filters)


def conv_kernel(got_ref, y_ref, vf, ff, yf, lhs, rhs):
    count = SEQ * ROWS
    total_rows = count * CH
    vf[0:LANES, :] = jnp.zeros((LANES, LANES), F32)
    ff[0:CH, :] = jnp.zeros((CH, LANES), F32)
    half = ROWS * CH
    vf[LANES:, :] = got_ref[:, 0:half, :].astype(F32).reshape(total_rows, LANES)
    ff[CH:, :] = got_ref[:, half:, :].astype(F32).reshape(total_rows, LANES)
    row = lax.broadcasted_iota(jnp.int32, (LANES, LANES), 0)
    col = lax.broadcasted_iota(jnp.int32, (LANES, LANES), 1)
    keep = col >= row

    def turned(m, ch):
        line = ff[pl.ds(CH * m + CH + ch, 1), :]
        return pltpu.roll(jnp.broadcast_to(line, (LANES, LANES)), 0, 1, stride=1, stride_axis=0)

    def one(ch, _):
        for e in range(8):
            shifted = vf[pl.ds(LANES + ch - 16 * e, count, stride=CH), :]
            lhs[:, e * LANES:(e + 1) * LANES] = shifted.astype(BF16)
        before = turned(-1, ch)
        total = None
        for a in range(count // 16):
            for e in range(8):
                for odd in range(2):
                    now = turned(16 * a + 2 * e + odd, ch)
                    rhs[a % 2, e * LANES:(e + 1) * LANES, odd * LANES:(odd + 1) * LANES] = (
                        jnp.where(keep, now, before).astype(BF16))
                    before = now
            part = jnp.dot(lhs[0:count - 16 * a, :], rhs[a % 2], preferred_element_type=F32)
            if a:
                part = total + jnp.concatenate([jnp.zeros((16 * a, 2 * LANES), F32), part], 0)
            total = part
        yf[pl.ds(ch, count, stride=CH), :] = total[:, :LANES]
        yf[pl.ds(ch + CH, count - 1, stride=CH), :] += total[:count - 1, LANES:]
        return 0

    lax.fori_loop(0, CH, one, 0)
    y_ref[...] = yf[...].astype(BF16).reshape(SEQ, half, LANES)


def conv(got):
    count = SEQ * ROWS
    return pl.pallas_call(
        conv_kernel,
        out_shape=jax.ShapeDtypeStruct((SEQ, ROWS * CH, LANES), BF16),
        in_specs=[pl.BlockSpec(memory_space=VMEM)],
        out_specs=pl.BlockSpec(memory_space=VMEM),
        scratch_shapes=[
            VMEM((count * CH + LANES, LANES), F32),
            VMEM((count * CH + CH, LANES), F32),
            VMEM((count * CH, LANES), F32),
            VMEM((count, 8 * LANES), BF16),
            VMEM((2, 8 * LANES, 2 * LANES), BF16),
        ],
        compiler_params=pltpu.CompilerParams(vmem_limit_bytes=24 * 2**20),
        cost_estimate=pl.CostEstimate(
            flops=2 * CH * 2 * count * LANES * count * LANES, bytes_accessed=2**20, transcendentals=0),
        name="convolve",
    )(got)


def project_kernel(y_ref, v_ref, g_ref, skip_ref, w_ref, o_ref,
                   back, mix, weight, psend, pgot,
                   ssem, rsem, wssem, wrsem, mssem, mrsem, pssem, prsem):
    me, x, z, c = seq_coords()
    chan = lax.axis_index("chan")
    y, l = lax.div(chan, NL), mod(chan, NL)
    barrier = pltpu.get_barrier_semaphore()

    def hello(k, _):
        signal(barrier, mod(me + k, SEQ), chan)
        return 0

    lax.fori_loop(1, SEQ, hello, 0)
    for d in range(1, 4):
        signal(barrier, me, mod(y + d, NY) * NL + l)
        signal(barrier, me, y * NL + mod(l + d, NL))
    pl.semaphore_wait(barrier, SEQ - 1 + 6)

    def partner(dz, j):
        dx, dc = lax.div(j, NC), mod(j, NC)
        return seq_id(mod(x + dx, NX), mod(z + dz, NZ), mod(c + dc, NC))

    for dz in (2, 1, 3, 0):
        def send(j, _, dz=dz):
            to = partner(dz, j)
            remote(y_ref.at[to], back.at[me], ssem.at[to], rsem.at[me], to, chan).start()
            return 0

        lax.fori_loop(0 if dz else 1, NX * NC, send, 0)

    mine = x * NC + c

    def weight_copy(j, slot):
        dx, dc = lax.div(j, NC), mod(j, NC)
        to = seq_id(mod(x + dx, NX), z, mod(c + dc, NC))
        return remote(w_ref, weight.at[slot], wssem.at[j], wrsem.at[slot], to, chan)

    def send_weight(j, _):
        weight_copy(j, mine).start()
        return 0

    lax.fori_loop(1, NX * NC, send_weight, 0)
    weight[mine] = w_ref[...]
    back[me] = y_ref[me]

    def mix_copy(d, g, slot):
        rows = pl.ds(pl.multiple_of(16 * g, 16), 16)
        return remote(mix.at[slot, rows], mix.at[slot, rows], mssem.at[d - 1, g], mrsem.at[d - 1, g],
                      me, mod(y + d, NY) * NL + l)

    def blend(g):
        rows = pl.ds(pl.multiple_of(16 * g, 16), 16)
        first, second = back[2 * g].astype(F32), back[2 * g + 1].astype(F32)
        for p in range(ROWS):
            cols = slice(LANES * p, LANES * (p + 1))
            filtered = jnp.concatenate([first[CH * p:CH * (p + 1)], second[CH * p:CH * (p + 1)]], 0)
            value, gate = v_ref[rows, cols].astype(F32), g_ref[rows, cols].astype(F32)
            mix[y, rows, cols] = (gate * (filtered + skip_ref[rows, :] * value)).astype(BF16)
        for d in (2, 1, 3):
            mix_copy(d, g, y).start()

    def arrive(src):
        remote(y_ref.at[src], back.at[src], ssem.at[src], rsem.at[src], src, chan).wait()

    for dz in (0, 1, 3, 2):
        def step(dx, _, dz=dz):
            g = mod(x + dx, NX) * NZ + mod(z + dz, NZ)
            arrive(2 * g)
            arrive(2 * g + 1)
            blend(g)
            return 0

        if dz == 0:
            arrive(seq_id(x, z, 1 - c))
            blend(x * NZ + z)
        lax.fori_loop(0 if dz else 1, NX, step, 0)

    def weight_done(j, _):
        dx, dc = lax.div(j, NC), mod(j, NC)
        source = mod(x - dx + NX, NX) * NC + mod(c + dc, NC)
        weight_copy(j, source).wait()
        return 0

    lax.fori_loop(1, NX * NC, weight_done, 0)

    for d in (1, 3, 2):
        def mixed_done(g, _, d=d):
            mix_copy(d, g, mod(y - d + NY, NY)).wait()
            return 0

        lax.fori_loop(0, SEQ // 2, mixed_done, 0)

    def product(o):
        t = mod(z - o + NZ, NZ)
        left = jnp.concatenate([weight[j, t] for j in range(NX * NC)], 1)
        right = mix[...].reshape(NY * 2 * LANES, ROWS * LANES)
        return jnp.dot(left, right, preferred_element_type=F32)

    def partial_copy(d):
        return remote(psend.at[d - 1], pgot.at[d - 1], pssem.at[d - 1], prsem.at[d - 1],
                      me, y * NL + mod(l + d, NL))

    for d in (2, 1, 3):
        psend[d - 1] = product(mod(l + d, NL)).astype(BF16)
        partial_copy(d).start()
    total = product(l)
    for d in (1, 3, 2):
        partial_copy(d).wait()
    for d in (1, 3, 2):
        total = total + pgot[d - 1].astype(F32)
    o_ref[...] = total.astype(BF16)


def project(y, values, gates, skip, w):
    tokens = ROWS * LANES
    block = 2 * LANES
    return pl.pallas_call(
        project_kernel,
        out_shape=jax.ShapeDtypeStruct((block, tokens), BF16),
        in_specs=[pl.BlockSpec(memory_space=VMEM)] * 5,
        out_specs=pl.BlockSpec(memory_space=VMEM),
        scratch_shapes=[
            VMEM((SEQ, ROWS * CH, LANES), BF16),
            VMEM((NY, block, tokens), BF16),
            VMEM((NX * NC, NL, block, LANES), BF16),
            VMEM((3, block, tokens), BF16),
            VMEM((3, block, tokens), BF16),
            pltpu.SemaphoreType.DMA((SEQ,)),
            pltpu.SemaphoreType.DMA((SEQ,)),
            pltpu.SemaphoreType.DMA((NX * NC,)),
            pltpu.SemaphoreType.DMA((NX * NC,)),
            pltpu.SemaphoreType.DMA((3, SEQ // 2)),
            pltpu.SemaphoreType.DMA((3, SEQ // 2)),
            pltpu.SemaphoreType.DMA((3,)),
            pltpu.SemaphoreType.DMA((3,)),
        ],
        compiler_params=pltpu.CompilerParams(
            collective_id=2, has_side_effects=True, vmem_limit_bytes=32 * 2**20),
        name="mix_and_project",
    )(y, values, gates, skip, w)


def weight_route(turn):
    pairs = []
    for x in range(NX):
        for b in range(NZ):
            for c in range(NC):
                for y in range(NY):
                    for l in range(NL):
                        source = (x * NZ * NC + b * NC + c) * NY * NL + y * NL + l
                        target = (x * NZ * NC + (l + turn) % NZ * NC + c) * NY * NL + y * NL + b
                        pairs.append((source, target))
    return pairs


def per_device(values, gates, skip_gain, filters, out_weight):
    got = scatter(values, filters)
    turned = out_weight.T
    routed = jnp.stack([lax.ppermute(turned, ("seq", "chan"), weight_route(t)) for t in range(NZ)])
    y = conv(got)
    return project(y, values, gates, skip_gain[:, None], routed)


def solution(mesh):
    return jax.shard_map(
        per_device,
        mesh=mesh,
        in_specs=(
            P("chan", "seq"),
            P("chan", "seq"),
            P("chan"),
            P("chan", "seq"),
            P("seq", "chan"),
        ),
        out_specs=P("chan", "seq"),
        check_vma=False,
    )
```

```python
import functools

import jax
import jax.numpy as jnp
from jax import lax
from jax.experimental import pallas as pl
from jax.experimental.pallas import tpu as pltpu
from jax.sharding import PartitionSpec as P

MESH = pl.DeviceIdType.MESH
VMEM = pltpu.VMEM
BF16 = jnp.bfloat16
F32 = jnp.float32

NX, NZ, NC = 4, 4, 2
SEQ = NX * NZ * NC
NY, NL = 4, 4
LANES = 128
ROWS = 4
PARTS = 2
CH = 4
TOKENS = ROWS * LANES
BLOCK = PARTS * CH * SEQ
COUNT = SEQ * ROWS
BOX = ROWS * CH


def mod(a, n):
    return lax.rem(a, n)


def seq_coords():
    s = lax.axis_index("seq")
    return s, lax.div(s, NZ * NC), mod(lax.div(s, NC), NZ), mod(s, NC)


def seq_id(x, z, c):
    return x * (NZ * NC) + z * NC + c


def signal(sem, seq, chan):
    pl.semaphore_signal(sem, inc=1, device_id={"seq": seq, "chan": chan}, device_id_type=MESH)


def remote(src, dst, ssem, rsem, seq, chan):
    return pltpu.make_async_remote_copy(
        src_ref=src, dst_ref=dst, send_sem=ssem, recv_sem=rsem,
        device_id={"seq": seq, "chan": chan}, device_id_type=MESH)


def halves(x, y):
    low = lax.broadcasted_iota(jnp.int32, (8, LANES), 0) < CH
    return jnp.where(low, x, pltpu.roll(y, CH, 0)), jnp.where(low, pltpu.roll(x, CH, 0), y)


def convolve(load, vf, ff, yf, lhs, rhs):
    vf[0:LANES, :] = jnp.zeros((LANES, LANES), F32)
    ff[0:CH, :] = jnp.zeros((CH, LANES), F32)
    load()
    row = lax.broadcasted_iota(jnp.int32, (LANES, LANES), 0)
    col = lax.broadcasted_iota(jnp.int32, (LANES, LANES), 1)
    keep = col >= row

    def turned(m, ch):
        line = ff[pl.ds(CH * m + CH + ch, 1), :]
        return pltpu.roll(jnp.broadcast_to(line, (LANES, LANES)), 0, 1, stride=1, stride_axis=0)

    def one(ch, _):
        for e in range(8):
            shifted = vf[pl.ds(LANES + ch - 2 * CH * e, COUNT, stride=CH), :]
            lhs[:, e * LANES:(e + 1) * LANES] = shifted.astype(BF16)
        before = turned(-1, ch)
        total = None
        for a in range(COUNT // 16):
            for e in range(8):
                for odd in range(2):
                    now = turned(16 * a + 2 * e + odd, ch)
                    rhs[a % 2, e * LANES:(e + 1) * LANES, odd * LANES:(odd + 1) * LANES] = (
                        jnp.where(keep, now, before).astype(BF16))
                    before = now
            part = jnp.dot(lhs[0:COUNT - 16 * a, :], rhs[a % 2], preferred_element_type=F32)
            if a:
                part = total + jnp.concatenate([jnp.zeros((16 * a, 2 * LANES), F32), part], 0)
            total = part
        yf[pl.ds(ch, COUNT, stride=CH), :] = total[:, :LANES]
        yf[pl.ds(ch + CH, COUNT - 1, stride=CH), :] += total[:COUNT - 1, LANES:]
        return 0

    lax.fori_loop(0, CH, one, 0)


def block_kernel(v_hbm, f_hbm, g_hbm, skip_ref, w_hbm, o_ref,
                 v_ref, f_ref, g_ref, w_ref, out, got, vf, ff, yf, lhs, rhs, done, back, mix, wt, weight,
                 psend, pgot, lsem, ssem, rsem, bssem, brsem, w1s, w1r, w2s, w2r, w3s, w3r,
                 mssem, mrsem, pssem, prsem):
    me, x, z, c = seq_coords()
    chan = lax.axis_index("chan")
    y, l = lax.div(chan, NL), mod(chan, NL)
    barrier = pltpu.get_barrier_semaphore()

    local = [pltpu.make_async_copy(a, b, lsem.at[i])
             for i, (a, b) in enumerate(((v_hbm, v_ref), (f_hbm, f_ref), (w_hbm, w_ref), (g_hbm, g_ref)))]
    for copy in local:
        copy.start()

    def hello(k, _):
        signal(barrier, mod(me + k, SEQ), chan)
        return 0

    lax.fori_loop(1, SEQ, hello, 0)
    for d in range(1, 4):
        signal(barrier, me, mod(y + d, NY) * NL + l)
        signal(barrier, me, y * NL + mod(l + d, NL))
    for t in range(1, NZ):
        signal(barrier, seq_id(x, l, c), y * NL + mod(z - t + NZ, NZ))

    @pl.when(l != z)
    def _():
        signal(barrier, seq_id(x, l, c), y * NL + z)

    def partner(dz, j):
        dx, dc = lax.div(j, NC), mod(j, NC)
        return seq_id(mod(x + dx, NX), mod(z + dz, NZ), mod(c + dc, NC))

    def each_partner(body, order=(2, 1, 3, 0)):
        for dz in order:
            def step(j, _, dz=dz):
                body(partner(dz, j))
                return 0

            lax.fori_loop(0 if dz else 1, NX * NC, step, 0)

    def pack(q):
        def step(h, _):
            rows = pl.ds(pl.multiple_of(BLOCK // PARTS * q + 16 * h, 16), 16)
            for ref, base in ((v_ref, 0), (f_ref, BOX)):
                block = ref[rows, :].astype(F32)
                for u in range(2):
                    p = [block[8 * u:8 * u + 8, LANES * i:LANES * (i + 1)] for i in range(ROWS)]
                    first, second = halves(p[0], p[1]), halves(p[2], p[3])
                    for odd in range(2):
                        out[q, 4 * h + 2 * u + odd, base:base + BOX, :] = jnp.concatenate(
                            [first[odd], second[odd]], 0).astype(BF16)
            return 0

        lax.fori_loop(0, SEQ // 4, step, 0)

    def scatter_copy(q, to, slot):
        return remote(out.at[q, to], got.at[q, slot], ssem.at[q, to], rsem.at[q, slot], to, chan)

    def return_copy(q, to, slot):
        return remote(done.at[q, to], back.at[q, slot], bssem.at[q, to], brsem.at[q, slot], to, chan)

    local[0].wait()
    local[1].wait()
    pack(0)
    pl.semaphore_wait(barrier, SEQ - 1 + 6 + 3 + jnp.where(l == z, 0, 1))
    each_partner(lambda to: scatter_copy(0, to, me).start())
    pack(1)
    each_partner(lambda to: scatter_copy(1, to, me).start())
    got[0, me] = out[0, me]
    got[1, me] = out[1, me]
    local[2].wait()
    wt[...] = w_ref[...].astype(F32).T.astype(BF16)
    local[3].wait()

    mine = x * NC + c

    def weight_copy(t):
        return remote(wt, weight.at[mine, t], w1s.at[t], w1r.at[t],
                      seq_id(x, mod(l + t, NZ), c), y * NL + z)

    for q in range(PARTS):
        each_partner(lambda to: scatter_copy(q, to, to).wait_recv())
        if q == 0:
            for t in range(1, NZ):
                weight_copy(t).start()

            @pl.when(l != z)
            def _():
                weight_copy(0).start()

            @pl.when(l == z)
            def _():
                weight[mine, 0] = wt[...]

        def load(q=q):
            vf[LANES:, :] = got[q, :, 0:BOX, :].astype(F32).reshape(COUNT * CH, LANES)
            ff[CH:, :] = got[q, :, BOX:, :].astype(F32).reshape(COUNT * CH, LANES)

        convolve(load, vf, ff, yf, lhs, rhs)
        done[q] = yf[...].astype(BF16).reshape(SEQ, BOX, LANES)
        each_partner(lambda to: return_copy(q, to, me).start())
        back[q, me] = done[q, me]

    for t in range(1, NZ):
        weight_copy(t).wait()

    @pl.when(l != z)
    def _():
        weight_copy(0).wait()

    def across_copy(d, slot):
        return remote(weight.at[slot], weight.at[slot], w2s.at[d - 1], w2r.at[d - 1],
                      seq_id(mod(x + d, NX), z, c), chan)

    def core_copy(d, slot):
        return remote(weight.at[slot], weight.at[slot], w3s.at[d], w3r.at[d], seq_id(x, z, 1 - c), chan)

    for d in (2, 1, 3):
        across_copy(d, mine).start()
    core_copy(0, mine).start()

    def mix_copy(d, b, slot):
        rows = pl.ds(pl.multiple_of(16 * b, 16), 16)
        return remote(mix.at[slot, rows], mix.at[slot, rows], mssem.at[d - 1, b], mrsem.at[d - 1, b],
                      me, mod(y + d, NY) * NL + l)

    def blend(q, h):
        start = pl.multiple_of(BLOCK // PARTS * q + 16 * h, 16)
        rows = pl.ds(start, 16)
        filtered = [[], [], [], []]
        for u in range(2):
            even, odd = back[q, 4 * h + 2 * u].astype(F32), back[q, 4 * h + 2 * u + 1].astype(F32)
            for i in range(2):
                pair = halves(even[8 * i:8 * i + 8], odd[8 * i:8 * i + 8])
                filtered[2 * i].append(pair[0])
                filtered[2 * i + 1].append(pair[1])
        for i in range(ROWS):
            cols = slice(LANES * i, LANES * (i + 1))
            value, gate = v_ref[rows, cols].astype(F32), g_ref[rows, cols].astype(F32)
            total = jnp.concatenate(filtered[i], 0) + skip_ref[rows, :] * value
            mix[y, rows, cols] = (gate * total).astype(BF16)
        for d in (2, 1, 3):
            mix_copy(d, (SEQ // 4) * q + h, y).start()

    for q in range(PARTS):
        for dz in range(2):
            def step(dx, _, dz=dz, q=q):
                h = mod(x + dx, NX) * 2 + mod(lax.div(z, 2) + dz, 2)
                for i in range(4):
                    src = 4 * h + i

                    @pl.when(src != me)
                    def _():
                        return_copy(q, src, src).wait_recv()

                blend(q, h)
                return 0

            lax.fori_loop(0, NX, step, 0)
        if q == 0:
            for d in (1, 3, 2):
                slot = mod(x - d + NX, NX) * NC + c
                across_copy(d, slot).wait()
                core_copy(d, slot).start()

    for d in range(NX):
        core_copy(d, mod(x - d + NX, NX) * NC + 1 - c).wait()

    for d in (1, 3, 2):
        def mixed_done(b, _, d=d):
            mix_copy(d, b, mod(y - d + NY, NY)).wait()
            return 0

        lax.fori_loop(0, BLOCK // 16, mixed_done, 0)

    def product(o):
        t = mod(z - o + NZ, NZ)
        left = jnp.concatenate([weight[j, t] for j in range(NX * NC)], 1)
        right = mix[...].reshape(NY * BLOCK, TOKENS)
        return jnp.dot(left, right, preferred_element_type=F32)

    def partial_copy(d):
        return remote(psend.at[d - 1], pgot.at[d - 1], pssem.at[d - 1], prsem.at[d - 1],
                      me, y * NL + mod(l + d, NL))

    for d in (2, 1, 3):
        psend[d - 1] = product(mod(l + d, NL)).astype(BF16)
        partial_copy(d).start()
    total = product(l)
    for q in range(PARTS):
        each_partner(lambda to: scatter_copy(q, to, me).wait_send())
        each_partner(lambda to: return_copy(q, to, me).wait_send())
    for d in (1, 3, 2):
        partial_copy(d).wait()
    for d in (1, 3, 2):
        total = total + pgot[d - 1].astype(F32)
    o_ref[...] = total.astype(BF16)


def per_device(values, gates, skip_gain, filters, out_weight):
    dma = pltpu.SemaphoreType.DMA
    hbm = pl.BlockSpec(memory_space=pl.ANY)
    vmem = pl.BlockSpec(memory_space=VMEM)
    return pl.pallas_call(
        block_kernel,
        out_shape=jax.ShapeDtypeStruct((BLOCK, TOKENS), BF16),
        in_specs=[hbm, hbm, hbm, vmem, hbm],
        out_specs=vmem,
        scratch_shapes=[
            VMEM((BLOCK, TOKENS), BF16), VMEM((BLOCK, TOKENS), BF16), VMEM((BLOCK, TOKENS), BF16),
            VMEM((LANES, BLOCK), BF16),
            VMEM((PARTS, SEQ, 2 * BOX, LANES), BF16), VMEM((PARTS, SEQ, 2 * BOX, LANES), BF16),
            VMEM((COUNT * CH + LANES, LANES), F32), VMEM((COUNT * CH + CH, LANES), F32),
            VMEM((COUNT * CH, LANES), F32),
            VMEM((COUNT, 8 * LANES), BF16), VMEM((2, 8 * LANES, 2 * LANES), BF16),
            VMEM((PARTS, SEQ, BOX, LANES), BF16), VMEM((PARTS, SEQ, BOX, LANES), BF16),
            VMEM((NY, BLOCK, TOKENS), BF16),
            VMEM((BLOCK, LANES), BF16), VMEM((NX * NC, NL, BLOCK, LANES), BF16),
            VMEM((3, BLOCK, TOKENS), BF16), VMEM((3, BLOCK, TOKENS), BF16),
            dma((4,)), dma((PARTS, SEQ)), dma((PARTS, SEQ)), dma((PARTS, SEQ)), dma((PARTS, SEQ)),
            dma((NZ,)), dma((NZ,)), dma((3,)), dma((3,)), dma((NX,)), dma((NX,)),
            dma((3, BLOCK // 16)), dma((3, BLOCK // 16)), dma((3,)), dma((3,)),
        ],
        compiler_params=pltpu.CompilerParams(
            collective_id=1, has_side_effects=True, vmem_limit_bytes=40 * 2**20),
        name="hyena_block",
    )(values, filters, gates, skip_gain[:, None], out_weight)


def solution(mesh):
    return jax.shard_map(
        per_device,
        mesh=mesh,
        in_specs=(
            P("chan", "seq"),
            P("chan", "seq"),
            P("chan"),
            P("chan", "seq"),
            P("seq", "chan"),
        ),
        out_specs=P("chan", "seq"),
        check_vma=False,
    )
```

```python
import functools

import jax
import jax.numpy as jnp
from jax import lax
from jax.experimental import pallas as pl
from jax.experimental.pallas import tpu as pltpu
from jax.sharding import PartitionSpec as P

MESH = pl.DeviceIdType.MESH
VMEM = pltpu.VMEM
BF16 = jnp.bfloat16
F32 = jnp.float32

NX, NZ, NC = 4, 4, 2
SEQ = NX * NZ * NC
NY, NL = 4, 4
LANES = 128
ROWS = 4
PARTS = 2
CH = 4
TOKENS = ROWS * LANES
BLOCK = PARTS * CH * SEQ
COUNT = SEQ * ROWS
BOX = ROWS * CH


def mod(a, n):
    return lax.rem(a, n)


def seq_coords():
    s = lax.axis_index("seq")
    return s, lax.div(s, NZ * NC), mod(lax.div(s, NC), NZ), mod(s, NC)


def seq_id(x, z, c):
    return x * (NZ * NC) + z * NC + c


def signal(sem, seq, chan):
    pl.semaphore_signal(sem, inc=1, device_id={"seq": seq, "chan": chan}, device_id_type=MESH)


def remote(src, dst, ssem, rsem, seq, chan):
    return pltpu.make_async_remote_copy(
        src_ref=src, dst_ref=dst, send_sem=ssem, recv_sem=rsem,
        device_id={"seq": seq, "chan": chan}, device_id_type=MESH)


def halves(x, y):
    low = lax.broadcasted_iota(jnp.int32, (8, LANES), 0) < CH
    return jnp.where(low, x, pltpu.roll(y, CH, 0)), jnp.where(low, pltpu.roll(x, CH, 0), y)


def convolve(load, vf, ff, yf, lhs, rhs, acc):
    vf[0:LANES, :] = jnp.zeros((LANES, LANES), F32)
    ff[0:CH, :] = jnp.zeros((CH, LANES), F32)
    load()
    half = LANES // 2
    row = lax.broadcasted_iota(jnp.int32, (half, LANES), 0)
    col = lax.broadcasted_iota(jnp.int32, (half, LANES), 1)
    keep = col >= row
    low = lax.broadcasted_iota(jnp.int32, (COUNT, LANES), 1) < half

    def turned(m, ch):
        line = ff[pl.ds(CH * m + CH + ch, 1), :]
        return pltpu.roll(jnp.broadcast_to(line, (half, LANES)), 0, 1, stride=1, stride_axis=0)

    def one(ch, _):
        for e in range(0, 8, 2):
            a, b = (vf[pl.ds(LANES + ch - 2 * CH * i, COUNT, stride=CH), :] for i in (e, e + 1))
            cols = slice(e * half, (e + 2) * half)
            lhs[0, :, cols] = jnp.where(low, a, pltpu.roll(b, half, 1)).astype(BF16)
            lhs[1, :, cols] = jnp.where(low, pltpu.roll(a, half, 1), b).astype(BF16)
        before = turned(-1, ch)
        for a in range(COUNT // 16):
            for e in range(8):
                for odd in range(2):
                    now = turned(16 * a + 2 * e + odd, ch)
                    rhs[a % 2, e * half:(e + 1) * half, odd * LANES:(odd + 1) * LANES] = (
                        jnp.where(keep, now, before).astype(BF16))
                    before = now
            rows = COUNT - 16 * a
            left = lhs[:, 0:rows, :].reshape(2 * rows, 8 * half)
            part = jnp.dot(left, rhs[a % 2], preferred_element_type=F32).reshape(2, rows, 2 * LANES)
            if a:
                acc[:, 16 * a:, :] += part
            else:
                acc[...] = part
        first, second = pltpu.roll(acc[1, :, :LANES], half, 1), pltpu.roll(acc[1, :, LANES:], half, 1)
        yf[pl.ds(ch, COUNT, stride=CH), :] = acc[0, :, :LANES] + jnp.where(low, 0.0, first)
        later = acc[0, :, LANES:] + jnp.where(low, first, second)
        yf[pl.ds(ch + CH, COUNT - 1, stride=CH), :] += later[:COUNT - 1]
        yf[pl.ds(ch + 2 * CH, COUNT - 2, stride=CH), :] += jnp.where(low, second, 0.0)[:COUNT - 2]
        return 0

    lax.fori_loop(0, CH, one, 0)


def block_kernel(v_hbm, f_hbm, g_hbm, s_hbm, w_hbm, o_ref,
                 v_ref, f_ref, g_ref, s_ref, w_ref, skip, out, got, vf, ff, yf, lhs, rhs, cacc, done, back, mix, early, weight,
                 acc, psend, pgot, lsem, ssem, rsem, bssem, brsem, w1s, w1r, w2s, w2r, w3s, w3r,
                 mssem, mrsem, cssem, crsem, pssem, prsem):
    me, x, z, c = seq_coords()
    chan = lax.axis_index("chan")
    y, l = lax.div(chan, NL), mod(chan, NL)
    barrier = pltpu.get_barrier_semaphore()

    local = [pltpu.make_async_copy(a, b, lsem.at[i])
             for i, (a, b) in enumerate(((v_hbm, v_ref), (f_hbm, f_ref), (w_hbm, w_ref), (g_hbm, g_ref), (s_hbm, s_ref)))]
    for copy in local:
        copy.start()

    def hello(k, _):
        signal(barrier, mod(me + k, SEQ), chan)
        return 0

    lax.fori_loop(1, SEQ, hello, 0)
    for d in range(1, 4):
        signal(barrier, me, mod(y + d, NY) * NL + l)
        signal(barrier, me, y * NL + mod(l + d, NL))
    for t in range(1, NX):
        signal(barrier, seq_id(y, z, c), mod(x - t + NX, NX) * NL + l)

    @pl.when(x != y)
    def _():
        signal(barrier, seq_id(y, z, c), x * NL + l)

    def partner(dz, j):
        dx, dc = lax.div(j, NC), mod(j, NC)
        return seq_id(mod(x + dx, NX), mod(z + dz, NZ), mod(c + dc, NC))

    def each_partner(body, order=(2, 1, 3, 0)):
        for dz in order:
            def step(j, _, dz=dz):
                body(partner(dz, j))
                return 0

            lax.fori_loop(0 if dz else 1, NX * NC, step, 0)

    def pack(q):
        def step(h, _):
            rows = pl.ds(pl.multiple_of(BLOCK // PARTS * q + 16 * h, 16), 16)
            for ref, base in ((v_ref, 0), (f_ref, BOX)):
                block = ref[rows, :].astype(F32)
                for u in range(2):
                    p = [block[8 * u:8 * u + 8, LANES * i:LANES * (i + 1)] for i in range(ROWS)]
                    first, second = halves(p[0], p[1]), halves(p[2], p[3])
                    for odd in range(2):
                        out[q, 4 * h + 2 * u + odd, base:base + BOX, :] = jnp.concatenate(
                            [first[odd], second[odd]], 0).astype(BF16)
            return 0

        lax.fori_loop(0, SEQ // 4, step, 0)

    def scatter_copy(q, to, slot):
        return remote(out.at[q, to], got.at[q, slot], ssem.at[q, to], rsem.at[q, slot], to, chan)

    def return_copy(q, to, slot):
        return remote(done.at[q, to], back.at[q, slot], bssem.at[q, to], brsem.at[q, slot], to, chan)

    local[0].wait()
    local[1].wait()
    pack(0)
    local[2].wait()
    early[z] = w_ref[...].astype(F32).T.astype(BF16)

    def weight_copy(i, slot):
        ref = early.at[slot] if i < 2 else early.at[slot, pl.ds(LANES * (i - 2), LANES)]
        return remote(ref, ref, w1s.at[i], w1r.at[i], seq_id(x, mod(z + (3 if i % 2 else 1), NZ), c), chan)

    def across_copy(b, t):
        return remote(early.at[b], weight.at[c, t, b], w2s.at[b, t], w2r.at[b, t],
                      seq_id(mod(y + t, NX), z, c), x * NL + l)

    def send_across(b):
        for t in range(1, NX):
            across_copy(b, t).start()

        @pl.when(x != y)
        def _():
            across_copy(b, 0).start()

        @pl.when(x == y)
        def _():
            weight[c, 0, b] = early[b]

    def relay_weights():
        for i, slot in ((0, mod(z + 3, NZ)), (1, mod(z + 1, NZ))):
            weight_copy(i, slot).wait()
            weight_copy(2 + i, slot).start()
            send_across(slot)

    def finish_weights():
        slot = mod(z + 2, NZ)
        weight_copy(2, slot).wait()
        weight_copy(3, slot).wait()
        send_across(slot)

    def share_weights():
        for b in range(NZ):
            for t in range(1, NX):
                across_copy(b, t).wait()

            @pl.when(x != y)
            def _():
                across_copy(b, 0).wait()

        for t in range(NX):
            core_copy(t, c).start()

    def core_copy(t, half):
        return remote(weight.at[half, t], weight.at[half, t], w3s.at[t], w3r.at[t],
                      seq_id(x, z, 1 - c), chan)

    pl.semaphore_wait(barrier, SEQ - 1 + 6 + 3 + jnp.where(x == y, 0, 1))
    each_partner(lambda to: scatter_copy(0, to, me).start())
    pack(1)
    each_partner(lambda to: scatter_copy(1, to, me).start())
    weight_copy(0, z).start()
    weight_copy(1, z).start()
    send_across(z)
    got[0, me] = out[0, me]
    got[1, me] = out[1, me]
    local[3].wait()
    local[4].wait()
    for q in range(BLOCK // LANES):
        line = s_ref[:, LANES * q:LANES * (q + 1)]
        skip[LANES * q:LANES * (q + 1), :] = jnp.broadcast_to(line, (LANES, LANES)).T

    for q in range(PARTS):
        each_partner(lambda to: scatter_copy(q, to, to).wait_recv())
        if q == 0:
            relay_weights()

        def load(q=q):
            vf[LANES:, :] = got[q, :, 0:BOX, :].astype(F32).reshape(COUNT * CH, LANES)
            ff[CH:, :] = got[q, :, BOX:, :].astype(F32).reshape(COUNT * CH, LANES)

        convolve(load, vf, ff, yf, lhs, rhs, cacc)
        done[q] = yf[...].astype(BF16).reshape(SEQ, BOX, LANES)
        each_partner(lambda to: return_copy(q, to, me).start())
        back[q, me] = done[q, me]

    pieces = ((0, 0, ROWS), (1, 0, ROWS // 2), (1, ROWS // 2, ROWS))

    def piece_at(k, h):
        q, first, last = pieces[k]
        rows = pl.ds(pl.multiple_of(BLOCK // PARTS * q + 16 * h, 16), 16)
        return rows, slice(LANES * first, LANES * last)

    def mix_copy(d, k, h, slot):
        ref = mix.at[(slot,) + piece_at(k, h)]
        b = SEQ // 4 * (k - 1) + h
        return remote(ref, ref, mssem.at[d - 1, b], mrsem.at[d - 1, b], me, y * NL + mod(l + d, NL))

    def blend(k, h):
        q, first, last = pieces[k]
        rows, _ = piece_at(k, h)
        filtered = [[], [], [], []]
        for u in range(2):
            even, odd = back[q, 4 * h + 2 * u].astype(F32), back[q, 4 * h + 2 * u + 1].astype(F32)
            for i in range(first // 2, last // 2):
                pair = halves(even[8 * i:8 * i + 8], odd[8 * i:8 * i + 8])
                filtered[2 * i].append(pair[0])
                filtered[2 * i + 1].append(pair[1])
        for i in range(first, last):
            cols = slice(LANES * i, LANES * (i + 1))
            value, gate = v_ref[rows, cols].astype(F32), g_ref[rows, cols].astype(F32)
            total = jnp.concatenate(filtered[i], 0) + skip[rows, :] * value
            mix[l, rows, cols] = (gate * total).astype(BF16)
        if k:
            for d in (2, 1, 3):
                mix_copy(d, k, h, l).start()

    def chain_copy(slot, way):
        ref = mix.at[slot, pl.ds(0, BLOCK // PARTS)]
        return remote(ref, ref, cssem.at[slot, way], crsem.at[slot], me,
                      y * NL + mod(l + (3 if way else 1), NL))

    def on_chain(j, body):
        @pl.when(l >= j)
        def _():
            body(mod(l - j + NL, NL), 0)

        @pl.when(l < NL - j)
        def _():
            body(mod(l + j, NL), 1)

    def pass_on(slot, way):
        @pl.when(l > 0 if way else l < NL - 1)
        def _():
            chain_copy(slot, way).start()

    def relay(slot, way):
        chain_copy(slot, way).wait_recv()
        pass_on(slot, way)

    def sent(slot, way):
        @pl.when(l > 0 if way else l < NL - 1)
        def _():
            chain_copy(slot, way).wait_send()

    for k in range(len(pieces)):
        q, first, _ = pieces[k]
        if k == 1:
            pass_on(l, 0)
            pass_on(l, 1)
            on_chain(1, relay)
            finish_weights()
            on_chain(2, relay)
        for dz in range(2):
            def step(dx, _, dz=dz, q=q, k=k, first=first):
                h = mod(x + dx, NX) * 2 + mod(lax.div(z, 2) + dz, 2)
                if first == 0:
                    for i in range(4):
                        src = 4 * h + i

                        @pl.when(src != me)
                        def _():
                            return_copy(q, src, src).wait_recv()

                blend(k, h)
                return 0

            lax.fori_loop(0, NX, step, 0)
    share_weights()

    def gathered(k):
        for d in (1, 3, 2):
            def step(h, _, d=d):
                mix_copy(d, k, h, mod(l - d + NL, NL)).wait()
                return 0

            lax.fori_loop(0, SEQ // 4, step, 0)

    def product(o, k):
        q, first, last = pieces[k]
        t = mod(x - o + NX, NX)
        left = jnp.concatenate([weight[q, t, b] for b in range(NL)], 1)
        half = BLOCK // PARTS
        right = mix[:, half * q:half * (q + 1), LANES * first:LANES * last]
        return jnp.dot(left, right.reshape(NL * half, LANES * (last - first)), preferred_element_type=F32)

    def partial_copy(d, k):
        return remote(psend.at[d - 1, k - 1], pgot.at[d - 1, k - 1], pssem.at[d - 1, k - 1],
                      prsem.at[d - 1, k - 1], me, mod(y + d, NY) * NL + l)

    for t in range(NX):
        core_copy(t, 1 - c).wait()
    on_chain(3, lambda slot, way: chain_copy(slot, way).wait_recv())
    sent(l, 0)
    sent(l, 1)
    on_chain(1, sent)
    on_chain(2, sent)
    for d in range(NY):
        acc[d] = product(mod(y + d, NY), 0)
    for k in (1, 2):
        cols = slice(LANES * pieces[k][1], LANES * pieces[k][2])
        gathered(k)
        for d in (2, 1, 3):
            psend[d - 1, k - 1] = (acc[d, :, cols] + product(mod(y + d, NY), k)).astype(BF16)
            partial_copy(d, k).start()
        acc[0, :, cols] += product(y, k)
    for q in range(PARTS):
        each_partner(lambda to: scatter_copy(q, to, me).wait_send())
        each_partner(lambda to: return_copy(q, to, me).wait_send())
    for k in (1, 2):
        cols = slice(LANES * pieces[k][1], LANES * pieces[k][2])
        total = acc[0, :, cols]
        for d in (1, 3, 2):
            partial_copy(d, k).wait()
            total = total + pgot[d - 1, k - 1].astype(F32)
        o_ref[:, cols] = total.astype(BF16)


def per_device(values, gates, skip_gain, filters, out_weight):
    dma = pltpu.SemaphoreType.DMA
    hbm = pl.BlockSpec(memory_space=pltpu.HBM)
    vmem = pl.BlockSpec(memory_space=VMEM)
    return pl.pallas_call(
        block_kernel,
        out_shape=jax.ShapeDtypeStruct((BLOCK, TOKENS), BF16),
        in_specs=[hbm, hbm, hbm, hbm, hbm],
        out_specs=vmem,
        scratch_shapes=[
            VMEM((BLOCK, TOKENS), BF16), VMEM((BLOCK, TOKENS), BF16), VMEM((BLOCK, TOKENS), BF16),
            VMEM((1, BLOCK), F32), VMEM((LANES, BLOCK), BF16), VMEM((BLOCK, LANES), F32),
            VMEM((PARTS, SEQ, 2 * BOX, LANES), BF16), VMEM((PARTS, SEQ, 2 * BOX, LANES), BF16),
            VMEM((COUNT * CH + LANES, LANES), F32), VMEM((COUNT * CH + CH, LANES), F32),
            VMEM((COUNT * CH, LANES), F32),
            VMEM((2, COUNT, 4 * LANES), BF16), VMEM((2, 4 * LANES, 2 * LANES), BF16),
            VMEM((2, COUNT, 2 * LANES), F32),
            VMEM((PARTS, SEQ, BOX, LANES), BF16), VMEM((PARTS, SEQ, BOX, LANES), BF16),
            VMEM((NL, BLOCK, TOKENS), BF16),
            VMEM((NZ, BLOCK, LANES), BF16), VMEM((NC, NX, NZ, BLOCK, LANES), BF16),
            VMEM((NY, BLOCK, TOKENS), F32),
            VMEM((3, 2, BLOCK, TOKENS // 2), BF16), VMEM((3, 2, BLOCK, TOKENS // 2), BF16),
            dma((5,)), dma((PARTS, SEQ)), dma((PARTS, SEQ)), dma((PARTS, SEQ)), dma((PARTS, SEQ)),
            dma((4,)), dma((4,)), dma((NZ, NX)), dma((NZ, NX)), dma((NX,)), dma((NX,)),
            dma((3, SEQ // 2)), dma((3, SEQ // 2)), dma((NL, 2)), dma((NL,)), dma((3, 2)), dma((3, 2)),
        ],
        compiler_params=pltpu.CompilerParams(
            collective_id=1, has_side_effects=True, vmem_limit_bytes=64 * 2**20),
        name="hyena_block",
    )(values, filters, gates, skip_gain[None], out_weight)


def solution(mesh):
    return jax.shard_map(
        per_device,
        mesh=mesh,
        in_specs=(
            P("chan", "seq"),
            P("chan", "seq"),
            P("chan"),
            P("chan", "seq"),
            P("seq", "chan"),
        ),
        out_specs=P("chan", "seq"),
        check_vma=False,
    )
```

```python
import functools

import jax
import jax.numpy as jnp
from jax import lax
from jax.experimental import pallas as pl
from jax.experimental.pallas import tpu as pltpu
from jax.sharding import PartitionSpec as P

MESH = pl.DeviceIdType.MESH
VMEM = pltpu.VMEM
BF16 = jnp.bfloat16
F32 = jnp.float32

NX, NZ, NC = 4, 4, 2
SEQ = NX * NZ * NC
NY, NL = 4, 4
LANES = 128
ROWS = 4
PARTS = 2
CH = 4
TOKENS = ROWS * LANES
BLOCK = PARTS * CH * SEQ
COUNT = SEQ * ROWS
BOX = ROWS * CH


def mod(a, n):
    return lax.rem(a, n)


def seq_coords():
    s = lax.axis_index("seq")
    return s, lax.div(s, NZ * NC), mod(lax.div(s, NC), NZ), mod(s, NC)


def seq_id(x, z, c):
    return x * (NZ * NC) + z * NC + c


def signal(sem, seq, chan):
    pl.semaphore_signal(sem, inc=1, device_id={"seq": seq, "chan": chan}, device_id_type=MESH)


def remote(src, dst, ssem, rsem, seq, chan):
    return pltpu.make_async_remote_copy(
        src_ref=src, dst_ref=dst, send_sem=ssem, recv_sem=rsem,
        device_id={"seq": seq, "chan": chan}, device_id_type=MESH)


def halves(x, y):
    low = lax.broadcasted_iota(jnp.int32, (8, LANES), 0) < CH
    return jnp.where(low, x, pltpu.roll(y, CH, 0)), jnp.where(low, pltpu.roll(x, CH, 0), y)


def convolve(load, vf, ff, yf, lhs, rhs, acc):
    vf[0:LANES, :] = jnp.zeros((LANES, LANES), F32)
    ff[0:CH, :] = jnp.zeros((CH, LANES), F32)
    load()
    half = LANES // 2
    row = lax.broadcasted_iota(jnp.int32, (half, LANES), 0)
    col = lax.broadcasted_iota(jnp.int32, (half, LANES), 1)
    keep = col >= row
    low = lax.broadcasted_iota(jnp.int32, (COUNT, LANES), 1) < half

    def turned(m, ch):
        line = ff[pl.ds(CH * m + CH + ch, 1), :]
        return pltpu.roll(jnp.broadcast_to(line, (half, LANES)), 0, 1, stride=1, stride_axis=0)

    def one(ch, _):
        for e in range(0, 8, 2):
            a, b = (vf[pl.ds(LANES + ch - 2 * CH * i, COUNT, stride=CH), :] for i in (e, e + 1))
            cols = slice(e * half, (e + 2) * half)
            lhs[0, :, cols] = jnp.where(low, a, pltpu.roll(b, half, 1)).astype(BF16)
            lhs[1, :, cols] = jnp.where(low, pltpu.roll(a, half, 1), b).astype(BF16)
        before = turned(-1, ch)
        for a in range(COUNT // 16):
            for e in range(8):
                for odd in range(2):
                    now = turned(16 * a + 2 * e + odd, ch)
                    rhs[a % 2, e * half:(e + 1) * half, odd * LANES:(odd + 1) * LANES] = (
                        jnp.where(keep, now, before).astype(BF16))
                    before = now
            rows = COUNT - 16 * a
            left = lhs[:, 0:rows, :].reshape(2 * rows, 8 * half)
            part = jnp.dot(left, rhs[a % 2], preferred_element_type=F32).reshape(2, rows, 2 * LANES)
            if a:
                acc[:, 16 * a:, :] += part
            else:
                acc[...] = part
        first, second = pltpu.roll(acc[1, :, :LANES], half, 1), pltpu.roll(acc[1, :, LANES:], half, 1)
        yf[pl.ds(ch, COUNT, stride=CH), :] = acc[0, :, :LANES] + jnp.where(low, 0.0, first)
        later = acc[0, :, LANES:] + jnp.where(low, first, second)
        yf[pl.ds(ch + CH, COUNT - 1, stride=CH), :] += later[:COUNT - 1]
        yf[pl.ds(ch + 2 * CH, COUNT - 2, stride=CH), :] += jnp.where(low, second, 0.0)[:COUNT - 2]
        return 0

    lax.fori_loop(0, CH, one, 0)


def block_kernel(v_hbm, f_hbm, g_hbm, s_hbm, w_hbm, o_ref,
                 v_ref, f_ref, g_ref, s_ref, w_ref, skip, out, got, vf, ff, yf, lhs, rhs, cacc, done, back, mix, early, weight,
                 acc, psend, pgot, lsem, ssem, rsem, bssem, brsem, w1s, w1r, w2s, w2r, w3s, w3r,
                 mssem, mrsem, cssem, crsem, pssem, prsem):
    me, x, z, c = seq_coords()
    chan = lax.axis_index("chan")
    y, l = lax.div(chan, NL), mod(chan, NL)
    barrier = pltpu.get_barrier_semaphore()

    local = [pltpu.make_async_copy(a, b, lsem.at[i])
             for i, (a, b) in enumerate(((v_hbm, v_ref), (f_hbm, f_ref), (w_hbm, w_ref), (g_hbm, g_ref), (s_hbm, s_ref)))]
    for copy in local:
        copy.start()

    def hello(k, _):
        signal(barrier, mod(me + k, SEQ), chan)
        return 0

    lax.fori_loop(1, SEQ, hello, 0)
    for d in range(1, 4):
        signal(barrier, me, mod(y + d, NY) * NL + l)
        signal(barrier, me, y * NL + mod(l + d, NL))
    for t in range(1, NX):
        signal(barrier, seq_id(y, z, c), mod(x - t + NX, NX) * NL + l)

    @pl.when(x != y)
    def _():
        signal(barrier, seq_id(y, z, c), x * NL + l)

    def partner(dz, j):
        dx, dc = lax.div(j, NC), mod(j, NC)
        return seq_id(mod(x + dx, NX), mod(z + dz, NZ), mod(c + dc, NC))

    def each_partner(body, order=(2, 1, 3, 0)):
        for dz in order:
            def step(j, _, dz=dz):
                body(partner(dz, j))
                return 0

            lax.fori_loop(0 if dz else 1, NX * NC, step, 0)

    def pack(q):
        def step(h, _):
            rows = pl.ds(pl.multiple_of(BLOCK // PARTS * q + 16 * h, 16), 16)
            for ref, base in ((v_ref, 0), (f_ref, BOX)):
                block = ref[rows, :].astype(F32)
                for u in range(2):
                    p = [block[8 * u:8 * u + 8, LANES * i:LANES * (i + 1)] for i in range(ROWS)]
                    first, second = halves(p[0], p[1]), halves(p[2], p[3])
                    for odd in range(2):
                        out[q, 4 * h + 2 * u + odd, base:base + BOX, :] = jnp.concatenate(
                            [first[odd], second[odd]], 0).astype(BF16)
            return 0

        lax.fori_loop(0, SEQ // 4, step, 0)

    def scatter_copy(q, to, slot):
        return remote(out.at[q, to], got.at[q, slot], ssem.at[q, to], rsem.at[q, slot], to, chan)

    def return_copy(q, to, slot):
        return remote(done.at[q, to], back.at[q, slot], bssem.at[q, to], brsem.at[q, slot], to, chan)

    local[0].wait()
    local[1].wait()
    pack(0)
    local[2].wait()
    early[z] = w_ref[...].astype(F32).T.astype(BF16)

    def weight_copy(i, slot):
        ref = early.at[slot] if i < 2 else early.at[slot, pl.ds(LANES * (i - 2), LANES)]
        return remote(ref, ref, w1s.at[i], w1r.at[i], seq_id(x, mod(z + (3 if i % 2 else 1), NZ), c), chan)

    def across_copy(b, t):
        return remote(early.at[b], weight.at[c, t, b], w2s.at[b, t], w2r.at[b, t],
                      seq_id(mod(y + t, NX), z, c), x * NL + l)

    def send_across(b):
        for t in range(1, NX):
            across_copy(b, t).start()

        @pl.when(x != y)
        def _():
            across_copy(b, 0).start()

        @pl.when(x == y)
        def _():
            weight[c, 0, b] = early[b]

    def relay_weights():
        for i, slot in ((0, mod(z + 3, NZ)), (1, mod(z + 1, NZ))):
            weight_copy(i, slot).wait()
            weight_copy(2 + i, slot).start()
            send_across(slot)

    def finish_weights():
        slot = mod(z + 2, NZ)
        weight_copy(2, slot).wait()
        weight_copy(3, slot).wait()
        send_across(slot)

    def share_weights():
        for b in range(NZ):
            for t in range(1, NX):
                across_copy(b, t).wait()

            @pl.when(x != y)
            def _():
                across_copy(b, 0).wait()

        for t in range(NX):
            core_copy(t, c).start()

    def core_copy(t, half):
        return remote(weight.at[half, t], weight.at[half, t], w3s.at[t], w3r.at[t],
                      seq_id(x, z, 1 - c), chan)

    pl.semaphore_wait(barrier, SEQ - 1 + 6 + 3 + jnp.where(x == y, 0, 1))
    each_partner(lambda to: scatter_copy(0, to, me).start())
    pack(1)
    each_partner(lambda to: scatter_copy(1, to, me).start())
    send_across(z)
    got[0, me] = out[0, me]
    got[1, me] = out[1, me]
    local[3].wait()
    local[4].wait()
    for q in range(BLOCK // LANES):
        line = s_ref[:, LANES * q:LANES * (q + 1)]
        skip[LANES * q:LANES * (q + 1), :] = jnp.broadcast_to(line, (LANES, LANES)).T

    for q in range(PARTS):
        each_partner(lambda to: scatter_copy(q, to, to).wait_recv())
        if q == 0:
            weight_copy(0, z).start()
            weight_copy(1, z).start()
        else:
            relay_weights()

        def load(q=q):
            vf[LANES:, :] = got[q, :, 0:BOX, :].astype(F32).reshape(COUNT * CH, LANES)
            ff[CH:, :] = got[q, :, BOX:, :].astype(F32).reshape(COUNT * CH, LANES)

        convolve(load, vf, ff, yf, lhs, rhs, cacc)
        done[q] = yf[...].astype(BF16).reshape(SEQ, BOX, LANES)
        each_partner(lambda to: return_copy(q, to, me).start())
        back[q, me] = done[q, me]

    pieces = ((0, 0, ROWS), (1, 0, ROWS // 2), (1, ROWS // 2, ROWS))

    def piece_at(k, h):
        q, first, last = pieces[k]
        rows = pl.ds(pl.multiple_of(BLOCK // PARTS * q + 16 * h, 16), 16)
        return rows, slice(LANES * first, LANES * last)

    def mix_copy(d, k, h, slot):
        ref = mix.at[(slot,) + piece_at(k, h)]
        b = SEQ // 4 * (k - 1) + h
        return remote(ref, ref, mssem.at[d - 1, b], mrsem.at[d - 1, b], me, y * NL + mod(l + d, NL))

    def blend(k, h):
        q, first, last = pieces[k]
        rows, _ = piece_at(k, h)
        filtered = [[], [], [], []]
        for u in range(2):
            even, odd = back[q, 4 * h + 2 * u].astype(F32), back[q, 4 * h + 2 * u + 1].astype(F32)
            for i in range(first // 2, last // 2):
                pair = halves(even[8 * i:8 * i + 8], odd[8 * i:8 * i + 8])
                filtered[2 * i].append(pair[0])
                filtered[2 * i + 1].append(pair[1])
        for i in range(first, last):
            cols = slice(LANES * i, LANES * (i + 1))
            value, gate = v_ref[rows, cols].astype(F32), g_ref[rows, cols].astype(F32)
            total = jnp.concatenate(filtered[i], 0) + skip[rows, :] * value
            mix[l, rows, cols] = (gate * total).astype(BF16)
        if k:
            for d in (2, 1, 3):
                mix_copy(d, k, h, l).start()

    def chain_copy(slot, way):
        ref = mix.at[slot, pl.ds(0, BLOCK // PARTS)]
        return remote(ref, ref, cssem.at[slot, way], crsem.at[slot], me,
                      y * NL + mod(l + (3 if way else 1), NL))

    def on_chain(j, body):
        @pl.when(l >= j)
        def _():
            body(mod(l - j + NL, NL), 0)

        @pl.when(l < NL - j)
        def _():
            body(mod(l + j, NL), 1)

    def pass_on(slot, way):
        @pl.when(l > 0 if way else l < NL - 1)
        def _():
            chain_copy(slot, way).start()

    def relay(slot, way):
        chain_copy(slot, way).wait_recv()
        pass_on(slot, way)

    def sent(slot, way):
        @pl.when(l > 0 if way else l < NL - 1)
        def _():
            chain_copy(slot, way).wait_send()

    for k in range(len(pieces)):
        q, first, _ = pieces[k]
        if k == 1:
            pass_on(l, 0)
            pass_on(l, 1)
            on_chain(1, relay)
            finish_weights()
            on_chain(2, relay)
        for dz in range(2):
            def step(dx, _, dz=dz, q=q, k=k, first=first):
                h = mod(x + dx, NX) * 2 + mod(lax.div(z, 2) + dz, 2)
                if first == 0:
                    for i in range(4):
                        src = 4 * h + i

                        @pl.when(src != me)
                        def _():
                            return_copy(q, src, src).wait_recv()

                blend(k, h)
                return 0

            lax.fori_loop(0, NX, step, 0)
    share_weights()

    def gathered(k):
        for d in (1, 3, 2):
            def step(h, _, d=d):
                mix_copy(d, k, h, mod(l - d + NL, NL)).wait()
                return 0

            lax.fori_loop(0, SEQ // 4, step, 0)

    def product(o, k):
        q, first, last = pieces[k]
        t = mod(x - o + NX, NX)
        left = jnp.concatenate([weight[q, t, b] for b in range(NL)], 1)
        half = BLOCK // PARTS
        right = mix[:, half * q:half * (q + 1), LANES * first:LANES * last]
        return jnp.dot(left, right.reshape(NL * half, LANES * (last - first)), preferred_element_type=F32)

    def partial_copy(d, k):
        return remote(psend.at[d - 1, k - 1], pgot.at[d - 1, k - 1], pssem.at[d - 1, k - 1],
                      prsem.at[d - 1, k - 1], me, mod(y + d, NY) * NL + l)

    for t in range(NX):
        core_copy(t, 1 - c).wait()
    on_chain(3, lambda slot, way: chain_copy(slot, way).wait_recv())
    sent(l, 0)
    sent(l, 1)
    on_chain(1, sent)
    on_chain(2, sent)
    for d in range(NY):
        acc[d] = product(mod(y + d, NY), 0)
    for k in (1, 2):
        cols = slice(LANES * pieces[k][1], LANES * pieces[k][2])
        gathered(k)
        for d in (2, 1, 3):
            psend[d - 1, k - 1] = (acc[d, :, cols] + product(mod(y + d, NY), k)).astype(BF16)
            partial_copy(d, k).start()
        acc[0, :, cols] += product(y, k)
    for q in range(PARTS):
        each_partner(lambda to: scatter_copy(q, to, me).wait_send())
        each_partner(lambda to: return_copy(q, to, me).wait_send())
    for k in (1, 2):
        cols = slice(LANES * pieces[k][1], LANES * pieces[k][2])
        total = acc[0, :, cols]
        for d in (1, 3, 2):
            partial_copy(d, k).wait()
            total = total + pgot[d - 1, k - 1].astype(F32)
        o_ref[:, cols] = total.astype(BF16)


def per_device(values, gates, skip_gain, filters, out_weight):
    dma = pltpu.SemaphoreType.DMA
    hbm = pl.BlockSpec(memory_space=pltpu.HBM)
    vmem = pl.BlockSpec(memory_space=VMEM)
    return pl.pallas_call(
        block_kernel,
        out_shape=jax.ShapeDtypeStruct((BLOCK, TOKENS), BF16),
        in_specs=[hbm, hbm, hbm, hbm, hbm],
        out_specs=vmem,
        scratch_shapes=[
            VMEM((BLOCK, TOKENS), BF16), VMEM((BLOCK, TOKENS), BF16), VMEM((BLOCK, TOKENS), BF16),
            VMEM((1, BLOCK), F32), VMEM((LANES, BLOCK), BF16), VMEM((BLOCK, LANES), F32),
            VMEM((PARTS, SEQ, 2 * BOX, LANES), BF16), VMEM((PARTS, SEQ, 2 * BOX, LANES), BF16),
            VMEM((COUNT * CH + LANES, LANES), F32), VMEM((COUNT * CH + CH, LANES), F32),
            VMEM((COUNT * CH, LANES), F32),
            VMEM((2, COUNT, 4 * LANES), BF16), VMEM((2, 4 * LANES, 2 * LANES), BF16),
            VMEM((2, COUNT, 2 * LANES), F32),
            VMEM((PARTS, SEQ, BOX, LANES), BF16), VMEM((PARTS, SEQ, BOX, LANES), BF16),
            VMEM((NL, BLOCK, TOKENS), BF16),
            VMEM((NZ, BLOCK, LANES), BF16), VMEM((NC, NX, NZ, BLOCK, LANES), BF16),
            VMEM((NY, BLOCK, TOKENS), F32),
            VMEM((3, 2, BLOCK, TOKENS // 2), BF16), VMEM((3, 2, BLOCK, TOKENS // 2), BF16),
            dma((5,)), dma((PARTS, SEQ)), dma((PARTS, SEQ)), dma((PARTS, SEQ)), dma((PARTS, SEQ)),
            dma((4,)), dma((4,)), dma((NZ, NX)), dma((NZ, NX)), dma((NX,)), dma((NX,)),
            dma((3, SEQ // 2)), dma((3, SEQ // 2)), dma((NL, 2)), dma((NL,)), dma((3, 2)), dma((3, 2)),
        ],
        compiler_params=pltpu.CompilerParams(
            collective_id=1, has_side_effects=True, vmem_limit_bytes=64 * 2**20),
        name="hyena_block",
    )(values, filters, gates, skip_gain[None], out_weight)


def solution(mesh):
    return jax.shard_map(
        per_device,
        mesh=mesh,
        in_specs=(
            P("chan", "seq"),
            P("chan", "seq"),
            P("chan"),
            P("chan", "seq"),
            P("seq", "chan"),
        ),
        out_specs=P("chan", "seq"),
        check_vma=False,
    )
```

```python
import functools

import jax
import jax.numpy as jnp
from jax import lax
from jax.experimental import pallas as pl
from jax.experimental.pallas import tpu as pltpu
from jax.sharding import PartitionSpec as P

MESH = pl.DeviceIdType.MESH
VMEM = pltpu.VMEM
BF16 = jnp.bfloat16
F32 = jnp.float32

NX, NZ, NC = 4, 4, 2
SEQ = NX * NZ * NC
NY, NL = 4, 4
LANES = 128
ROWS = 4
PARTS = 2
CH = 4
TOKENS = ROWS * LANES
BLOCK = PARTS * CH * SEQ
COUNT = SEQ * ROWS
BOX = ROWS * CH


def mod(a, n):
    return lax.rem(a, n)


def seq_coords():
    s = lax.axis_index("seq")
    return s, lax.div(s, NZ * NC), mod(lax.div(s, NC), NZ), mod(s, NC)


def seq_id(x, z, c):
    return x * (NZ * NC) + z * NC + c


def signal(sem, seq, chan):
    pl.semaphore_signal(sem, inc=1, device_id={"seq": seq, "chan": chan}, device_id_type=MESH)


def remote(src, dst, ssem, rsem, seq, chan):
    return pltpu.make_async_remote_copy(
        src_ref=src, dst_ref=dst, send_sem=ssem, recv_sem=rsem,
        device_id={"seq": seq, "chan": chan}, device_id_type=MESH)


def halves(x, y):
    low = lax.broadcasted_iota(jnp.int32, (8, LANES), 0) < CH
    return jnp.where(low, x, pltpu.roll(y, CH, 0)), jnp.where(low, pltpu.roll(x, CH, 0), y)


def convolve(load, vf, ff, yf, lhs, rhs, acc):
    vf[0:LANES, :] = jnp.zeros((LANES, LANES), F32)
    ff[0:CH, :] = jnp.zeros((CH, LANES), F32)
    load()
    half = LANES // 2
    row = lax.broadcasted_iota(jnp.int32, (half, LANES), 0)
    col = lax.broadcasted_iota(jnp.int32, (half, LANES), 1)
    keep = col >= row
    low = lax.broadcasted_iota(jnp.int32, (COUNT, LANES), 1) < half

    def turned(m, ch):
        line = ff[pl.ds(CH * m + CH + ch, 1), :]
        return pltpu.roll(jnp.broadcast_to(line, (half, LANES)), 0, 1, stride=1, stride_axis=0)

    def one(ch, _):
        for e in range(0, 8, 2):
            a, b = (vf[pl.ds(LANES + ch - 2 * CH * i, COUNT, stride=CH), :] for i in (e, e + 1))
            cols = slice(e * half, (e + 2) * half)
            lhs[0, :, cols] = jnp.where(low, a, pltpu.roll(b, half, 1)).astype(BF16)
            lhs[1, :, cols] = jnp.where(low, pltpu.roll(a, half, 1), b).astype(BF16)
        before = turned(-1, ch)
        for a in range(COUNT // 16):
            for e in range(8):
                for odd in range(2):
                    now = turned(16 * a + 2 * e + odd, ch)
                    rhs[a % 2, e * half:(e + 1) * half, odd * LANES:(odd + 1) * LANES] = (
                        jnp.where(keep, now, before).astype(BF16))
                    before = now
            rows = COUNT - 16 * a
            left = lhs[:, 0:rows, :].reshape(2 * rows, 8 * half)
            part = jnp.dot(left, rhs[a % 2], preferred_element_type=F32).reshape(2, rows, 2 * LANES)
            if a:
                acc[:, 16 * a:, :] += part
            else:
                acc[...] = part
        first, second = pltpu.roll(acc[1, :, :LANES], half, 1), pltpu.roll(acc[1, :, LANES:], half, 1)
        yf[pl.ds(ch, COUNT, stride=CH), :] = acc[0, :, :LANES] + jnp.where(low, 0.0, first)
        later = acc[0, :, LANES:] + jnp.where(low, first, second)
        yf[pl.ds(ch + CH, COUNT - 1, stride=CH), :] += later[:COUNT - 1]
        yf[pl.ds(ch + 2 * CH, COUNT - 2, stride=CH), :] += jnp.where(low, second, 0.0)[:COUNT - 2]
        return 0

    lax.fori_loop(0, CH, one, 0)


def block_kernel(v_hbm, f_hbm, g_hbm, s_hbm, w_hbm, o_ref,
                 v_ref, f_ref, g_ref, s_ref, w_ref, skip, out, got, vf, ff, yf, lhs, rhs, cacc, done, back, mix, early, weight,
                 acc, psend, pgot, lsem, ssem, rsem, bssem, brsem, w1s, w1r, w2s, w2r, w3s, w3r,
                 mssem, mrsem, cssem, crsem, pssem, prsem):
    me, x, z, c = seq_coords()
    chan = lax.axis_index("chan")
    y, l = lax.div(chan, NL), mod(chan, NL)
    barrier = pltpu.get_barrier_semaphore()

    local = [pltpu.make_async_copy(a, b, lsem.at[i])
             for i, (a, b) in enumerate(((v_hbm, v_ref), (f_hbm, f_ref), (w_hbm, w_ref), (g_hbm, g_ref), (s_hbm, s_ref)))]
    for copy in local:
        copy.start()

    def hello(k, _):
        signal(barrier, mod(me + k, SEQ), chan)
        return 0

    lax.fori_loop(1, SEQ, hello, 0)
    for d in range(1, 4):
        signal(barrier, me, mod(y + d, NY) * NL + l)
        signal(barrier, me, y * NL + mod(l + d, NL))
    for t in range(1, NX):
        signal(barrier, seq_id(y, z, c), mod(x - t + NX, NX) * NL + l)

    @pl.when(x != y)
    def _():
        signal(barrier, seq_id(y, z, c), x * NL + l)

    def partner(dz, j):
        dx, dc = lax.div(j, NC), mod(j, NC)
        return seq_id(mod(x + dx, NX), mod(z + dz, NZ), mod(c + dc, NC))

    def each_partner(body, order=(2, 1, 3, 0)):
        for dz in order:
            def step(j, _, dz=dz):
                body(partner(dz, j))
                return 0

            lax.fori_loop(0 if dz else 1, NX * NC, step, 0)

    def pack(q):
        def step(h, _):
            rows = pl.ds(pl.multiple_of(BLOCK // PARTS * q + 16 * h, 16), 16)
            for ref, base in ((v_ref, 0), (f_ref, BOX)):
                block = ref[rows, :].astype(F32)
                for u in range(2):
                    p = [block[8 * u:8 * u + 8, LANES * i:LANES * (i + 1)] for i in range(ROWS)]
                    first, second = halves(p[0], p[1]), halves(p[2], p[3])
                    for odd in range(2):
                        out[q, 4 * h + 2 * u + odd, base:base + BOX, :] = jnp.concatenate(
                            [first[odd], second[odd]], 0).astype(BF16)
            return 0

        lax.fori_loop(0, SEQ // 4, step, 0)

    def scatter_copy(q, to, slot):
        return remote(out.at[q, to], got.at[q, slot], ssem.at[q, to], rsem.at[q, slot], to, chan)

    def return_copy(q, to, slot):
        return remote(done.at[q, to], back.at[q, slot], bssem.at[q, to], brsem.at[q, slot], to, chan)

    local[0].wait()
    local[1].wait()
    pack(0)
    local[2].wait()
    early[z] = w_ref[...].astype(F32).T.astype(BF16)

    def weight_copy(i, slot):
        ref = early.at[slot] if i < 2 else early.at[slot, pl.ds(LANES * (i - 2), LANES)]
        return remote(ref, ref, w1s.at[i], w1r.at[i], seq_id(x, mod(z + (3 if i % 2 else 1), NZ), c), chan)

    def across_copy(b, t):
        return remote(early.at[b], weight.at[c, t, b], w2s.at[b, t], w2r.at[b, t],
                      seq_id(mod(y + t, NX), z, c), x * NL + l)

    def send_across(b):
        for t in range(1, NX):
            across_copy(b, t).start()

        @pl.when(x != y)
        def _():
            across_copy(b, 0).start()

        @pl.when(x == y)
        def _():
            weight[c, 0, b] = early[b]

    def relay_weights():
        for i, slot in ((0, mod(z + 3, NZ)), (1, mod(z + 1, NZ))):
            weight_copy(i, slot).wait()
            weight_copy(2 + i, slot).start()
            send_across(slot)

    def finish_weights():
        slot = mod(z + 2, NZ)
        weight_copy(2, slot).wait()
        weight_copy(3, slot).wait()
        send_across(slot)

    def share_weights():
        for b in range(NZ):
            for t in range(1, NX):
                across_copy(b, t).wait()

            @pl.when(x != y)
            def _():
                across_copy(b, 0).wait()

        for t in range(NX):
            core_copy(t, c).start()

    def core_copy(t, half):
        return remote(weight.at[half, t], weight.at[half, t], w3s.at[t], w3r.at[t],
                      seq_id(x, z, 1 - c), chan)

    pl.semaphore_wait(barrier, SEQ - 1 + 6 + 3 + jnp.where(x == y, 0, 1))
    each_partner(lambda to: scatter_copy(0, to, me).start())
    pack(1)
    each_partner(lambda to: scatter_copy(1, to, me).start())
    send_across(z)
    got[0, me] = out[0, me]
    got[1, me] = out[1, me]
    local[3].wait()
    local[4].wait()
    for q in range(BLOCK // LANES):
        line = s_ref[:, LANES * q:LANES * (q + 1)]
        skip[LANES * q:LANES * (q + 1), :] = jnp.broadcast_to(line, (LANES, LANES)).T

    for q in range(PARTS):
        each_partner(lambda to: scatter_copy(q, to, to).wait_recv())
        if q == 0:
            weight_copy(0, z).start()
            weight_copy(1, z).start()

        def load(q=q):
            vf[LANES:, :] = got[q, :, 0:BOX, :].astype(F32).reshape(COUNT * CH, LANES)
            ff[CH:, :] = got[q, :, BOX:, :].astype(F32).reshape(COUNT * CH, LANES)

        convolve(load, vf, ff, yf, lhs, rhs, cacc)
        done[q] = yf[...].astype(BF16).reshape(SEQ, BOX, LANES)
        each_partner(lambda to: return_copy(q, to, me).start())
        back[q, me] = done[q, me]

    relay_weights()

    pieces = ((0, 0, ROWS), (1, 0, ROWS // 2), (1, ROWS // 2, ROWS))

    def piece_at(k, h):
        q, first, last = pieces[k]
        rows = pl.ds(pl.multiple_of(BLOCK // PARTS * q + 16 * h, 16), 16)
        return rows, slice(LANES * first, LANES * last)

    def mix_copy(d, k, h, slot):
        ref = mix.at[(slot,) + piece_at(k, h)]
        b = SEQ // 4 * (k - 1) + h
        return remote(ref, ref, mssem.at[d - 1, b], mrsem.at[d - 1, b], me, y * NL + mod(l + d, NL))

    def blend(k, h):
        q, first, last = pieces[k]
        rows, _ = piece_at(k, h)
        filtered = [[], [], [], []]
        for u in range(2):
            even, odd = back[q, 4 * h + 2 * u].astype(F32), back[q, 4 * h + 2 * u + 1].astype(F32)
            for i in range(first // 2, last // 2):
                pair = halves(even[8 * i:8 * i + 8], odd[8 * i:8 * i + 8])
                filtered[2 * i].append(pair[0])
                filtered[2 * i + 1].append(pair[1])
        for i in range(first, last):
            cols = slice(LANES * i, LANES * (i + 1))
            value, gate = v_ref[rows, cols].astype(F32), g_ref[rows, cols].astype(F32)
            total = jnp.concatenate(filtered[i], 0) + skip[rows, :] * value
            mix[l, rows, cols] = (gate * total).astype(BF16)
        if k:
            for d in (2, 1, 3):
                mix_copy(d, k, h, l).start()

    def chain_copy(slot, way):
        ref = mix.at[slot, pl.ds(0, BLOCK // PARTS)]
        return remote(ref, ref, cssem.at[slot, way], crsem.at[slot], me,
                      y * NL + mod(l + (3 if way else 1), NL))

    def on_chain(j, body):
        @pl.when(l >= j)
        def _():
            body(mod(l - j + NL, NL), 0)

        @pl.when(l < NL - j)
        def _():
            body(mod(l + j, NL), 1)

    def pass_on(slot, way):
        @pl.when(l > 0 if way else l < NL - 1)
        def _():
            chain_copy(slot, way).start()

    def relay(slot, way):
        chain_copy(slot, way).wait_recv()
        pass_on(slot, way)

    def sent(slot, way):
        @pl.when(l > 0 if way else l < NL - 1)
        def _():
            chain_copy(slot, way).wait_send()

    for k in range(len(pieces)):
        q, first, _ = pieces[k]
        if k == 1:
            pass_on(l, 0)
            pass_on(l, 1)
            on_chain(1, relay)
            finish_weights()
            on_chain(2, relay)
        for dz in range(2):
            def step(dx, _, dz=dz, q=q, k=k, first=first):
                h = mod(x + dx, NX) * 2 + mod(lax.div(z, 2) + dz, 2)
                if first == 0:
                    for i in range(4):
                        src = 4 * h + i

                        @pl.when(src != me)
                        def _():
                            return_copy(q, src, src).wait_recv()

                blend(k, h)
                return 0

            lax.fori_loop(0, NX, step, 0)
    share_weights()

    def gathered(k):
        for d in (1, 3, 2):
            def step(h, _, d=d):
                mix_copy(d, k, h, mod(l - d + NL, NL)).wait()
                return 0

            lax.fori_loop(0, SEQ // 4, step, 0)

    def product(o, k):
        q, first, last = pieces[k]
        t = mod(x - o + NX, NX)
        left = jnp.concatenate([weight[q, t, b] for b in range(NL)], 1)
        half = BLOCK // PARTS
        right = mix[:, half * q:half * (q + 1), LANES * first:LANES * last]
        return jnp.dot(left, right.reshape(NL * half, LANES * (last - first)), preferred_element_type=F32)

    def partial_copy(d, k):
        return remote(psend.at[d - 1, k - 1], pgot.at[d - 1, k - 1], pssem.at[d - 1, k - 1],
                      prsem.at[d - 1, k - 1], me, mod(y + d, NY) * NL + l)

    for t in range(NX):
        core_copy(t, 1 - c).wait()
    on_chain(3, lambda slot, way: chain_copy(slot, way).wait_recv())
    sent(l, 0)
    sent(l, 1)
    on_chain(1, sent)
    on_chain(2, sent)
    for d in range(NY):
        acc[d] = product(mod(y + d, NY), 0)
    for k in (1, 2):
        cols = slice(LANES * pieces[k][1], LANES * pieces[k][2])
        gathered(k)
        for d in (2, 1, 3):
            psend[d - 1, k - 1] = (acc[d, :, cols] + product(mod(y + d, NY), k)).astype(BF16)
            partial_copy(d, k).start()
        acc[0, :, cols] += product(y, k)
    for q in range(PARTS):
        each_partner(lambda to: scatter_copy(q, to, me).wait_send())
        each_partner(lambda to: return_copy(q, to, me).wait_send())
    for k in (1, 2):
        cols = slice(LANES * pieces[k][1], LANES * pieces[k][2])
        total = acc[0, :, cols]
        for d in (1, 3, 2):
            partial_copy(d, k).wait()
            total = total + pgot[d - 1, k - 1].astype(F32)
        o_ref[:, cols] = total.astype(BF16)


def per_device(values, gates, skip_gain, filters, out_weight):
    dma = pltpu.SemaphoreType.DMA
    hbm = pl.BlockSpec(memory_space=pltpu.HBM)
    vmem = pl.BlockSpec(memory_space=VMEM)
    return pl.pallas_call(
        block_kernel,
        out_shape=jax.ShapeDtypeStruct((BLOCK, TOKENS), BF16),
        in_specs=[hbm, hbm, hbm, hbm, hbm],
        out_specs=vmem,
        scratch_shapes=[
            VMEM((BLOCK, TOKENS), BF16), VMEM((BLOCK, TOKENS), BF16), VMEM((BLOCK, TOKENS), BF16),
            VMEM((1, BLOCK), F32), VMEM((LANES, BLOCK), BF16), VMEM((BLOCK, LANES), F32),
            VMEM((PARTS, SEQ, 2 * BOX, LANES), BF16), VMEM((PARTS, SEQ, 2 * BOX, LANES), BF16),
            VMEM((COUNT * CH + LANES, LANES), F32), VMEM((COUNT * CH + CH, LANES), F32),
            VMEM((COUNT * CH, LANES), F32),
            VMEM((2, COUNT, 4 * LANES), BF16), VMEM((2, 4 * LANES, 2 * LANES), BF16),
            VMEM((2, COUNT, 2 * LANES), F32),
            VMEM((PARTS, SEQ, BOX, LANES), BF16), VMEM((PARTS, SEQ, BOX, LANES), BF16),
            VMEM((NL, BLOCK, TOKENS), BF16),
            VMEM((NZ, BLOCK, LANES), BF16), VMEM((NC, NX, NZ, BLOCK, LANES), BF16),
            VMEM((NY, BLOCK, TOKENS), F32),
            VMEM((3, 2, BLOCK, TOKENS // 2), BF16), VMEM((3, 2, BLOCK, TOKENS // 2), BF16),
            dma((5,)), dma((PARTS, SEQ)), dma((PARTS, SEQ)), dma((PARTS, SEQ)), dma((PARTS, SEQ)),
            dma((4,)), dma((4,)), dma((NZ, NX)), dma((NZ, NX)), dma((NX,)), dma((NX,)),
            dma((3, SEQ // 2)), dma((3, SEQ // 2)), dma((NL, 2)), dma((NL,)), dma((3, 2)), dma((3, 2)),
        ],
        compiler_params=pltpu.CompilerParams(
            collective_id=1, has_side_effects=True, vmem_limit_bytes=64 * 2**20),
        name="hyena_block",
    )(values, filters, gates, skip_gain[None], out_weight)


def solution(mesh):
    return jax.shard_map(
        per_device,
        mesh=mesh,
        in_specs=(
            P("chan", "seq"),
            P("chan", "seq"),
            P("chan"),
            P("chan", "seq"),
            P("seq", "chan"),
        ),
        out_specs=P("chan", "seq"),
        check_vma=False,
    )
```
